512 devices in a mesh: dp: 64 (over y, z_lo, core), mp: 8 (over z_hi, x).
Axes of the slice: x: 4, y: 8, z: 8 (z_hi: 2, z_lo: 4; z = z_hi * 4 + z_lo), core: 2. Of those that a mesh axis runs over, the one named last changes fastest.
Arguments:
- inputs: bfloat16 [131072, 3072], P(('dp', 'mp')), may hold values from -24 to 24
- weight: bfloat16 [3072, 384], P('dp', 'mp'), may hold values from -0.109375 to 0.109375
- d_out: bfloat16 [131072, 128], P(('dp', 'mp')), may hold values from -6 to 6
Outputs:
- grad_inputs: bfloat16 [131072, 3072], P(('dp', 'mp'))
- weight_grad: float32 [3072, 384], P('dp', 'mp')
The draws below stay inside these ranges and needn't reach their ends.
All inputs are finite; a program needn't handle non-finite values.
Results may differ from the reference program's by a relative error of at most 0.015.
Values may be sent and summed in bfloat16 or wider, within the bound.
A program may use at most 64 MiB of HBM per device.

```python
import jax
import jax.numpy as jnp
from jax import lax

D = 3072
HD = 128
SEQ = 256
TOKENS = 131072


def spiked(values, stream_key, source, target, shards_of, factor):
    def block_of(dim):
        return (jnp.arange(values.shape[dim]) // (values.shape[dim] // shards_of)).reshape((-1,) + (1,) * (values.ndim - 1 - dim))

    first = jax.random.permutation(stream_key, shards_of)[block_of(target)]
    other_side = (block_of(target) + shards_of // 2) % shards_of
    return jnp.where((block_of(source) == first) | (block_of(source) == other_side), factor * values, values)


def block_levels(stream_key, extent, split, low, largest):
    loudness, own = 1.0, jax.random.fold_in(stream_key, 6)
    for position, parts in split:
        heights = jnp.exp(jax.random.uniform(jax.random.fold_in(own, position), (parts,), jnp.float32, low / len(split), largest / len(split)))
        loudness = loudness * jnp.repeat(heights, extent[position] // parts).reshape([-1 if axis == position else 1 for axis in range(len(extent))])
    return loudness


def centred(stream_key, shape, scale, most, shards=(), kind=jnp.bfloat16):
    result = jax.random.normal(stream_key, shape, jnp.float32) * scale
    if len(shards) > 0:
        result = block_levels(stream_key, shape, shards, -0.22, 0.18) * result
    return jnp.clip(result, min=-most, max=most).astype(kind)


def gaussian_with(stream_key, extent, scale, reach, cuts, heavy, held_as=jnp.bfloat16):
    entries = scale * jax.random.normal(stream_key, extent, jnp.float32)
    if cuts:
        entries = entries * block_levels(stream_key, extent, cuts, -0.22, 0.18)
    return jnp.clip(spiked(entries, jax.random.fold_in(stream_key, 3), *heavy), -reach, reach).astype(held_as)


def setup_inputs(seed: int = 0) -> dict:
    arg_keys = jax.random.split(jax.random.key(seed), 4)
    return {
        "inputs": gaussian_with(arg_keys[0], (TOKENS, D), 1.0, 24.0, ((0, 512),), (0, 1, 512, 6.0)),
        "weight": centred(arg_keys[1], (D, 3 * HD), D ** -0.5, 0.109375, ((0, 64), (1, 8))),
        "d_out": centred(arg_keys[2], (TOKENS, HD), 1.0, 6.0, ((0, 512),)),
    }


def attend_back(qkv, d_out):
    hd = d_out.shape[1]
    blocks = qkv.astype(jnp.float32)
    query_rows = blocks[:, :hd]
    key_rows = blocks[:, hd:2 * hd]
    value_rows = blocks[:, 2 * hd:]
    gradient_list = d_out.astype(jnp.float32)
    scaling_factor = hd ** -0.5
    score_matrix = jnp.dot(query_rows, key_rows.T) * scaling_factor
    probs = jax.nn.softmax(score_matrix, axis=-1)
    probabilities_reduced = lax.optimization_barrier(probs.astype(jnp.bfloat16)).astype(jnp.float32)
    value_gradient = jnp.dot(probabilities_reduced.T, gradient_list)
    probability_gradient = jnp.dot(gradient_list, value_rows.T)
    delta = jnp.sum(probs * probability_gradient, axis=-1, keepdims=True)
    score_gradient = lax.optimization_barrier((probs * (probability_gradient - delta)).astype(jnp.bfloat16)).astype(jnp.float32)
    query_gradient = jnp.dot(score_gradient, key_rows) * scaling_factor
    key_gradient = jnp.dot(score_gradient.T, query_rows) * scaling_factor
    return jnp.concatenate([query_gradient, key_gradient, value_gradient], axis=-1).astype(jnp.bfloat16)


def reference(inputs, weight, d_out):
    width = inputs.shape[1]
    cols = weight.shape[1]
    images = inputs.shape[0] // SEQ
    rows_in = inputs.reshape(images, SEQ, width)
    rows_grad = d_out.reshape(images, SEQ, d_out.shape[1])

    def image(total, pair):
        tokens, gradient_list = pair
        qkv = jnp.dot(tokens, weight, preferred_element_type=jnp.float32).astype(jnp.bfloat16)
        grad_qkv = attend_back(qkv, gradient_list)
        grad_in = lax.dot_general(grad_qkv, weight, (((1,), (1,)), ((), ())), preferred_element_type=jnp.float32).astype(jnp.bfloat16)
        share = lax.dot_general(tokens, grad_qkv, (((0,), (0,)), ((), ())), preferred_element_type=jnp.float32)
        rounded = lax.optimization_barrier(share.astype(jnp.bfloat16)).astype(jnp.float32)
        return total + rounded, grad_in

    weight_grad, grad_inputs = lax.scan(image, jnp.zeros((width, cols), jnp.float32), (rows_in, rows_grad))
    return grad_inputs.reshape(images * SEQ, width), weight_grad
```

```python
import jax
import jax.numpy as jnp
from jax import lax
from jax.experimental import pallas as pl
from jax.experimental.pallas import tpu as pltpu
from jax.sharding import PartitionSpec as P

MESH = pl.DeviceIdType.MESH
BF = jnp.bfloat16
F32 = jnp.float32

NY, NZL, NC, NM = 8, 4, 2, 8
B = 48
CH = 384
STEPS = (0, 1, 7, 2, 6, 3, 5, 4)


def dot(a, b):
    return jnp.dot(a, b, preferred_element_type=F32)


def dot_nt(a, b):
    return lax.dot_general(a, b, (((1,), (1,)), ((), ())), preferred_element_type=F32)


def dot_tn(a, b):
    return lax.dot_general(a, b, (((0,), (0,)), ((), ())), preferred_element_type=F32)


def attention_back(qkv, d_out):
    hd = 128
    scale = hd**-0.5
    q, k, v = qkv[:, :hd], qkv[:, hd : 2 * hd], qkv[:, 2 * hd :]
    scores = dot_nt(q, k) * scale
    e = jnp.exp(scores - jnp.max(scores, axis=-1, keepdims=True))
    probs = e / jnp.sum(e, axis=-1, keepdims=True)
    grad_v = dot_tn(probs.astype(BF), d_out)
    grad_p = dot_nt(d_out, v)
    delta = jnp.sum(probs * grad_p, axis=-1, keepdims=True)
    grad_s = (probs * (grad_p - delta)).astype(BF)
    grad_q = dot(grad_s, k) * scale
    grad_k = dot_tn(grad_s, q) * scale
    return grad_q.astype(BF), grad_k.astype(BF), grad_v.astype(BF)


def kernel(
    inputs_hbm, weight, d_out, gi_hbm, wg_out,
    inputs, wm, w, acc, g_own, g_other, t_own, t_send, t_other,
    part, rz, s2, ry, sm, rm, gi,
    in_sem, gi_sem, wm_s, wm_r, y_s, y_r, z_s, z_r, c_s, c_r, t_s, t_r, g_s, g_r,
    rz_s, rz_r, ry_s, ry_r, rm_s, rm_r,
):
    dp, mp = lax.axis_index("dp"), lax.axis_index("mp")
    y, zl, c = dp // 8, (dp // 2) % 4, dp % 2
    zh, x = mp // 4, mp % 4
    z = zh * 4 + zl
    oc = 1 - c

    load = pltpu.make_async_copy(inputs_hbm, inputs, in_sem)
    load.start()

    def at(yy, zz, cc):
        return ((yy * 4 + zz % 4) * 2 + cc, (zz // 4) * 4 + x)

    def mp_peer(j):
        return (dp, (mp + j) % 8)

    def y_peer(d, cc):
        return at((y + d) % 8, z, cc)

    far = 2 - 4 * c
    z_steps = (1, -1, far)

    def z_peer(j, sign=1):
        return at(y, (z + sign * z_steps[j] + 8) % 8, c)

    core_peer = at(y, z, oc)

    wm[mp] = jnp.zeros((B, 128), BF)
    wm[mp, :, :B] = weight[...]

    barrier = pltpu.get_barrier_semaphore()
    peers = [mp_peer(j) for j in range(1, 8)]
    peers += [y_peer(d, c) for d in range(1, 8)]
    peers += [y_peer(d, oc) for d in range(0, 8)]
    peers += [at(y, (z + dz + 8) % 8, c) for dz in (1, -1, 2, -2)]
    for peer in peers:
        pl.semaphore_signal(barrier, inc=1, device_id=peer, device_id_type=MESH)
    pl.semaphore_wait(barrier, len(peers))

    def remote(src, dst, ssem, rsem, peer):
        return pltpu.make_async_remote_copy(
            src_ref=src, dst_ref=dst, send_sem=ssem, recv_sem=rsem,
            device_id=peer, device_id_type=MESH,
        )

    def wm_copy(j, slot):
        return remote(wm.at[slot], wm.at[slot], wm_s.at[j], wm_r.at[j], mp_peer(j))

    for j in range(1, 8):
        wm_copy(j, mp).start()

    load.wait()

    def chunk_of(k, half):
        return half * 4 + (k + y) % 4

    def columns(ch):
        return pl.ds(pl.multiple_of(ch * CH, CH), CH)

    for k in range(4):
        t_send[k] = inputs[:, columns(chunk_of(k, oc))].T
    t_copy = remote(t_send, t_other, t_s, t_r, core_peer)
    t_copy.start()

    for j in range(1, 8):
        wm_copy(j, (mp - j + 8) % 8).wait_recv()
    block = jnp.concatenate([wm[m, :, :B] for m in range(NM)], axis=1)
    w[y, zl, c] = block

    def y_copy(d, src_y):
        blk = w.at[src_y, zl, c]
        return remote(blk, blk, y_s.at[d], y_r.at[d], y_peer(d, c))

    def z_copy(k, j, src_y, src_zl):
        blk = w.at[src_y, src_zl, c]
        return remote(blk, blk, z_s.at[k, j], z_r.at[k, j], z_peer(j))

    def c_copy(k, src_y, cc):
        blk = w.at[src_y, :, cc]
        return remote(blk, blk, c_s.at[k], c_r.at[k], core_peer)

    for d in STEPS[1:]:
        y_copy(d, y).start()
    ys = [(y - d + 8) % 8 for d in STEPS]
    zls = [(zl - s + 8) % 4 for s in z_steps]
    for k in range(8):
        if k > 0:
            y_copy(STEPS[k], ys[k]).wait_recv()
        for j in (2, 0, 1):
            z_copy(k, j, ys[k], zl).start()
        if k < 4:
            t_own[k] = inputs[:, columns(chunk_of(k, c))].T

    def multiply(k):
        c_copy(k, ys[k], oc).wait_recv()
        p = dot(inputs[:, columns(ys[k])], w[ys[k]].reshape(CH, CH))
        if k == 0:
            acc[...] = p
        else:
            acc[...] += p

    for k in range(8):
        for j in range(3):
            z_copy(k, j, ys[k], zls[j]).wait_recv()
        c_copy(k, ys[k], c).start()
        if k > 0:
            multiply(k - 1)
    multiply(7)

    gq, gk, gv = attention_back(acc[...].astype(BF), d_out[...])
    g_own[:, :128] = gq
    g_own[:, 128:256] = gk
    g_own[:, 256:] = gv
    g_copy = remote(g_own, g_other, g_s, g_r, core_peer)
    g_copy.start()
    t_copy.wait_recv()
    g_copy.wait_recv()

    def rz_copy(k, j):
        to = (zl + z_steps[j] + 4) % 4
        return remote(
            part.at[k, to], rz.at[j, k], rz_s.at[k, j], rz_r.at[k, j], z_peer(j)
        )

    for k in range(4):
        p = dot(t_own[k], g_own[...]) + dot(t_other[k], g_other[...])
        part[k] = p.astype(BF).reshape(4, 2 * B, CH)
        for j in (2, 0, 1):
            rz_copy(k, j).start()

    def gi_copy(i):
        cols = pl.ds(i * CH, CH)
        return pltpu.make_async_copy(gi.at[:, cols], gi_hbm.at[:, cols], gi_sem.at[i])

    def ry_copy(k, cc):
        return remote(
            s2.at[k, cc], ry.at[y], ry_s.at[k, cc], ry_r.at[y],
            at(chunk_of(k, c), z, cc),
        )

    def is_self(k, cc):
        return jnp.logical_and(chunk_of(k, c) == y, cc == c)

    for k in range(4):
        for i in (2 * k, 2 * k + 1):
            gi[:, i * CH : (i + 1) * CH] = dot_nt(g_own[...], w[i].reshape(CH, CH)).astype(BF)
            gi_copy(i).start()
        for j in range(3):
            rz_copy(k, j).wait_recv()
        total = part[k, zl].astype(F32)
        for j in range(3):
            total += rz[j, k].astype(F32)
        s2[k] = total.astype(BF).reshape(2, B, CH)
        for cc in range(2):
            self_k = is_self(k, cc)

            @pl.when(self_k)
            def _():
                ry[y] = s2[k, cc]

            @pl.when(jnp.logical_not(self_k))
            def _():
                ry_copy(k, cc).start()

    src_core = y // 4
    for i in range(8):

        @pl.when(jnp.logical_not(jnp.logical_and(i == y, src_core == c)))
        def _():
            remote(s2.at[0, 0], ry.at[i], ry_s.at[0, 0], ry_r.at[i], core_peer).wait_recv()

    total = ry[0].astype(F32)
    for i in range(1, 8):
        total += ry[i].astype(F32)

    def rm_copy(j, to, slot):
        return remote(sm.at[to], rm.at[slot], rm_s.at[j], rm_r.at[j], mp_peer(j))

    for m in range(NM):
        sm[m, :, :B] = total[:, m * B : (m + 1) * B].astype(BF)
    for j in range(1, 8):
        rm_copy(j, (mp + j) % 8, mp).start()
    result = sm[mp, :, :B].astype(F32)
    for j in range(1, 8):
        rm_copy(j, 0, (mp - j + 8) % 8).wait_recv()
        result += rm[(mp - j + 8) % 8, :, :B].astype(F32)
    wg_out[...] = result

    for j in range(1, 8):
        wm_copy(j, mp).wait_send()
        y_copy(j, y).wait_send()
        rm_copy(j, 0, mp).wait_send()
    for k in range(8):
        for j in range(3):
            z_copy(k, j, ys[k], zl).wait_send()
        c_copy(k, ys[k], c).wait_send()
        gi_copy(k).wait()
    t_copy.wait_send()
    g_copy.wait_send()
    for k in range(4):
        for j in range(3):
            rz_copy(k, j).wait_send()
        for cc in range(2):

            @pl.when(jnp.logical_not(is_self(k, cc)))
            def _():
                ry_copy(k, cc).wait_send()


def per_device(inputs, weight, d_out):
    vmem, hbm = pl.BlockSpec(memory_space=pltpu.VMEM), pl.BlockSpec(memory_space=pl.ANY)
    dma = pltpu.SemaphoreType.DMA
    tokens, feats = inputs.shape
    return pl.pallas_call(
        kernel,
        out_shape=(
            jax.ShapeDtypeStruct((tokens, feats), BF),
            jax.ShapeDtypeStruct((B, B), F32),
        ),
        in_specs=[hbm, vmem, vmem],
        out_specs=(hbm, vmem),
        scratch_shapes=[
            pltpu.VMEM((tokens, feats), BF),
            pltpu.VMEM((NM, B, 128), BF),
            pltpu.VMEM((NY, NZL, NC, B, CH), BF),
            pltpu.VMEM((tokens, CH), F32),
            pltpu.VMEM((tokens, CH), BF),
            pltpu.VMEM((tokens, CH), BF),
            pltpu.VMEM((4, CH, tokens), BF),
            pltpu.VMEM((4, CH, tokens), BF),
            pltpu.VMEM((4, CH, tokens), BF),
            pltpu.VMEM((4, 4, 2 * B, CH), BF),
            pltpu.VMEM((3, 4, 2 * B, CH), BF),
            pltpu.VMEM((4, NC, B, CH), BF),
            pltpu.VMEM((NY, B, CH), BF),
            pltpu.VMEM((NM, B, 128), BF),
            pltpu.VMEM((NM, B, 128), BF),
            pltpu.VMEM((tokens, feats), BF),
            dma,
            dma((8,)),
            dma((8,)), dma((8,)),
            dma((8,)), dma((8,)),
            dma((8, 3)), dma((8, 3)),
            dma((8,)), dma((8,)),
            dma, dma,
            dma, dma,
            dma((4, 3)), dma((4, 3)),
            dma((4, 2)), dma((8,)),
            dma((8,)), dma((8,)),
        ],
        compiler_params=pltpu.CompilerParams(
            collective_id=0, has_side_effects=True, vmem_limit_bytes=40 << 20
        ),
        name="attention_head_back",
    )(inputs, weight, d_out)


def solution(mesh):
    in_specs = (P(("dp", "mp"), None), P("dp", "mp"), P(("dp", "mp"), None))
    out_specs = (P(("dp", "mp"), None), P("dp", "mp"))
    return jax.shard_map(
        per_device, mesh=mesh, in_specs=in_specs, out_specs=out_specs, check_vma=False
    )
```

```python
import jax
import jax.numpy as jnp
from jax import lax
from jax.experimental import pallas as pl
from jax.experimental.pallas import tpu as pltpu
from jax.sharding import PartitionSpec as P

MESH = pl.DeviceIdType.MESH
BF = jnp.bfloat16
F32 = jnp.float32

NY, NZL, NC, NM = 8, 4, 2, 8
B = 48
CH = 384
STEPS = (0, 1, 7, 2, 6, 3, 5, 4)


def dot(a, b):
    return jnp.dot(a, b, preferred_element_type=F32)


def dot_nt(a, b):
    return lax.dot_general(a, b, (((1,), (1,)), ((), ())), preferred_element_type=F32)


def dot_tn(a, b):
    return lax.dot_general(a, b, (((0,), (0,)), ((), ())), preferred_element_type=F32)


def attention_back(qkv, d_out):
    hd = 128
    scale = hd**-0.5
    q, k, v = qkv[:, :hd], qkv[:, hd : 2 * hd], qkv[:, 2 * hd :]
    scores = dot_nt(q, k) * scale
    e = jnp.exp(scores - jnp.max(scores, axis=-1, keepdims=True))
    probs = e / jnp.sum(e, axis=-1, keepdims=True)
    grad_v = dot_tn(probs.astype(BF), d_out)
    grad_p = dot_nt(d_out, v)
    delta = jnp.sum(probs * grad_p, axis=-1, keepdims=True)
    grad_s = (probs * (grad_p - delta)).astype(BF)
    grad_q = dot(grad_s, k) * scale
    grad_k = dot_tn(grad_s, q) * scale
    return grad_q.astype(BF), grad_k.astype(BF), grad_v.astype(BF)


def kernel(
    inputs_hbm, weight_hbm, d_out_hbm, gi, wg_out,
    inputs, weight, d_out, wm, w, acc, g_own, g_other, t_own, t_send, t_other,
    part, rx, sx, rz, s2, ry, sm, rm,
    in_sem, wm_s, wm_r, y_s, y_r, z_s, z_r, x_s, x_r, c_s, c_r, t_s, t_r, g_s, g_r,
    rx_s, rx_r, rz_s, rz_r, ry_s, ry_r, rm_s, rm_r,
):
    dp, mp = lax.axis_index("dp"), lax.axis_index("mp")
    y, zl, c = dp // 8, (dp // 2) % 4, dp % 2
    zh, x = mp // 4, mp % 4
    z = zh * 4 + zl
    oc = 1 - c

    load_w = pltpu.make_async_copy(weight_hbm, weight, in_sem.at[0])
    load_w.start()
    load = pltpu.make_async_copy(inputs_hbm, inputs, in_sem.at[1])
    load.start()
    load_d = pltpu.make_async_copy(d_out_hbm, d_out, in_sem.at[2])
    load_d.start()

    def at(yy, zz, cc):
        return ((yy * 4 + zz % 4) * 2 + cc, (zz // 4) * 4 + x)

    def mp_peer(j):
        return (dp, (mp + j) % 8)

    def y_peer(d, cc):
        return at((y + d) % 8, z, cc)

    far = 2 - 4 * c
    z_steps = (1, -1, far)

    def z_peer(j, sign=1):
        return at(y, (z + sign * z_steps[j] + 8) % 8, c)

    def x_peer(p):
        return (dp, zh * 4 + (x + p) % 4)

    core_peer = at(y, z, oc)

    barrier = pltpu.get_barrier_semaphore()
    peers = [mp_peer(j) for j in range(1, 8)]
    peers += [y_peer(d, c) for d in range(1, 8)]
    peers += [y_peer(d, oc) for d in range(0, 8)]
    peers += [at(y, (z + dz + 8) % 8, c) for dz in (1, -1, 2, -2)]
    for peer in peers:
        pl.semaphore_signal(barrier, inc=1, device_id=peer, device_id_type=MESH)
    load_w.wait()
    wm[mp] = jnp.zeros((B, 128), BF)
    wm[mp, :, :B] = weight[...]
    pl.semaphore_wait(barrier, len(peers))

    def remote(src, dst, ssem, rsem, peer):
        return pltpu.make_async_remote_copy(
            src_ref=src, dst_ref=dst, send_sem=ssem, recv_sem=rsem,
            device_id=peer, device_id_type=MESH,
        )

    def wm_copy(j, slot):
        return remote(wm.at[slot], wm.at[slot], wm_s.at[j], wm_r.at[j], mp_peer(j))

    for j in range(1, 8):
        wm_copy(j, mp).start()

    load.wait()
    load_d.wait()

    def chunk_of(k, half):
        return half * 4 + (k + y) % 4

    def columns(ch):
        return pl.ds(pl.multiple_of(ch * CH, CH), CH)

    for k in range(4):
        t_send[k] = inputs[:, columns(chunk_of(k, oc))].T
    t_copy = remote(t_send, t_other, t_s, t_r, core_peer)
    t_copy.start()

    for j in range(1, 8):
        wm_copy(j, (mp - j + 8) % 8).wait_recv()
    block = jnp.concatenate([wm[m, :, :B] for m in range(NM)], axis=1)
    w[y, zl, c] = block

    def y_copy(d, src_y):
        blk = w.at[src_y, zl, c]
        return remote(blk, blk, y_s.at[d], y_r.at[d], y_peer(d, c))

    def z_copy(k, j, src_y, src_zl):
        blk = w.at[src_y, src_zl, c]
        return remote(blk, blk, z_s.at[k, j], z_r.at[k, j], z_peer(j))

    def c_copy(k, src_y, cc):
        blk = w.at[src_y, :, cc]
        return remote(blk, blk, c_s.at[k], c_r.at[k], core_peer)

    def x_copy(p, j, src_y, src_zl):
        blk = w.at[src_y, src_zl, c]
        return remote(blk, blk, x_s.at[p, j], x_r.at[p, j], x_peer(p))

    for d in STEPS[1:]:
        y_copy(d, y).start()
    ys = [(y - d + 8) % 8 for d in STEPS]
    zls = [(zl - s + 8) % 4 for s in z_steps]

    def shared_y(xx):
        return (y - jnp.where(xx == 2, 7, jnp.where(xx == 3, 2, xx)) + 8) % 8

    my_shared = shared_y(x)
    for k in range(1, 4):

        @pl.when(x == k)
        def _():
            y_copy(STEPS[k], ys[k]).wait_recv()

    for j in (2, 0, 1):
        z_copy(0, j, my_shared, zl).start()
    for k in range(4, 8):
        y_copy(STEPS[k], ys[k]).wait_recv()
        for j in (2, 0, 1):
            z_copy(k, j, ys[k], zl).start()
    for k in range(1, 4):

        @pl.when(x != k)
        def _():
            y_copy(STEPS[k], ys[k]).wait_recv()

    for j in (0, 1, 2):
        z_copy(0, j, my_shared, zls[j]).wait_recv()
        for p in (2, 1, 3):
            x_copy(p, j, my_shared, zls[j]).start()
    for k in range(4):
        t_own[k] = inputs[:, columns(chunk_of(k, c))].T

    x_from = [(x - p + 4) % 4 for p in (1, 2, 3)]
    order = [(x, my_shared), (4, ys[4]), (5, ys[5])]
    order += [(xx, shared_y(xx)) for xx in x_from]
    order += [(6, ys[6]), (7, ys[7])]

    def multiply(n):
        k, yy = order[n]
        c_copy(k, yy, oc).wait_recv()
        p = dot(inputs[:, columns(yy)], w[yy].reshape(CH, CH))
        if n == 0:
            acc[...] = p
        else:
            acc[...] += p

    for n in range(8):
        k, yy = order[n]
        if n in (1, 2, 6, 7):
            for j in range(3):
                z_copy(k, j, yy, zls[j]).wait_recv()
        if n in (3, 4, 5):
            for j in range(3):
                x_copy(n - 2, j, yy, zls[j]).wait_recv()
        c_copy(k, yy, c).start()
        if n > 0:
            multiply(n - 1)
    multiply(7)

    gq, gk, gv = attention_back(acc[...].astype(BF), d_out[...])
    g_own[:, :128] = gq
    g_own[:, 128:256] = gk
    g_own[:, 256:] = gv
    g_copy = remote(g_own, g_other, g_s, g_r, core_peer)
    g_copy.start()
    t_copy.wait_recv()
    g_copy.wait_recv()

    dest_zl = [(zl + s + 4) % 4 for s in z_steps]
    owner = x // 2 == c
    mine = x % 2

    def rx_copy(k, p, j):
        to = dest_zl[j]
        return remote(
            part.at[k, to], rx.at[p, j], rx_s.at[k, j], rx_r.at[p, j], x_peer(p)
        )

    def rz_copy(k, j):
        src = sx.at[j] if k == 0 else part.at[k, dest_zl[j]]
        return remote(src, rz.at[j, k], rz_s.at[k, j], rz_r.at[k, j], z_peer(j))

    def ry_copy(k, cc):
        return remote(
            s2.at[k, cc], ry.at[y], ry_s.at[k, cc], ry_r.at[y],
            at(chunk_of(k, c), z, cc),
        )

    def is_self(k, cc):
        return jnp.logical_and(chunk_of(k, c) == y, cc == c)

    def send_y(k, total):
        s2[k] = total.reshape(2, B, CH)
        for cc in range(2):
            self_k = is_self(k, cc)

            @pl.when(self_k)
            def _():
                ry[y] = s2[k, cc]

            @pl.when(jnp.logical_not(self_k))
            def _():
                ry_copy(k, cc).start()

    for k in range(4):
        p = dot(t_own[k], g_own[...]) + dot(t_other[k], g_other[...])
        part[k] = p.astype(BF).reshape(4, 2 * B, CH)
        if k < 2:
            to_owner = (2 * c + k - x + 4) % 4

            @pl.when(to_owner != 0)
            def _():
                for j in (2, 0, 1):
                    rx_copy(k, to_owner, j).start()
        else:
            for j in (2, 0, 1):
                rz_copy(k, j).start()
    for k in range(2):

        @pl.when(x != 2 * c + k)
        def _():
            send_y(k, part[k, zl])

    def grad_inputs(i):
        gi[:, i * CH : (i + 1) * CH] = dot_nt(g_own[...], w[i].reshape(CH, CH)).astype(BF)

    for i in range(4):
        grad_inputs(i)
    for n, j in enumerate((2, 0, 1)):

        @pl.when(owner)
        def _():
            total = part[mine, dest_zl[j]].astype(F32)
            for p in (1, 2, 3):
                rx_copy(0, p, j).wait_recv()
                total += rx[p, j].astype(F32)
            sx[j] = total.astype(BF)
            rz_copy(0, j).start()

        grad_inputs(4 + n)
    grad_inputs(7)

    def from_z(k, total):
        for j in range(3):
            rz_copy(k, j).wait_recv()
            total += rz[j, k].astype(F32)
        return total.astype(BF)

    for k in (2, 3):
        send_y(k, from_z(k, part[k, zl].astype(F32)))

    @pl.when(owner)
    def _():
        total = from_z(0, part[mine, zl].astype(F32))
        for k in range(2):

            @pl.when(mine == k)
            def _():
                send_y(k, total)

    src_core = y // 4
    for i in range(8):

        @pl.when(jnp.logical_not(jnp.logical_and(i == y, src_core == c)))
        def _():
            remote(s2.at[0, 0], ry.at[i], ry_s.at[0, 0], ry_r.at[i], core_peer).wait_recv()

    total = ry[0].astype(F32)
    for i in range(1, 8):
        total += ry[i].astype(F32)

    def rm_copy(j, to, slot):
        return remote(sm.at[to], rm.at[slot], rm_s.at[j], rm_r.at[j], mp_peer(j))

    for m in range(NM):
        sm[m, :, :B] = total[:, m * B : (m + 1) * B].astype(BF)
    for j in range(1, 8):
        rm_copy(j, (mp + j) % 8, mp).start()
    result = sm[mp, :, :B].astype(F32)
    for j in range(1, 8):
        rm_copy(j, 0, (mp - j + 8) % 8).wait_recv()
        result += rm[(mp - j + 8) % 8, :, :B].astype(F32)
    wg_out[...] = result

    for j in range(1, 8):
        wm_copy(j, mp).wait_send()
        y_copy(j, y).wait_send()
        rm_copy(j, 0, mp).wait_send()
    for j in range(3):
        for k in (0, 4, 5, 6, 7):
            z_copy(k, j, ys[k], zl).wait_send()
        for p in (1, 2, 3):
            x_copy(p, j, y, zl).wait_send()
        for k in (2, 3):
            rz_copy(k, j).wait_send()
    for k in range(8):
        c_copy(k, ys[k], c).wait_send()
    t_copy.wait_send()
    g_copy.wait_send()

    @pl.when(owner)
    def _():
        for j in range(3):
            rz_copy(0, j).wait_send()

    for k in range(2):

        @pl.when(x != 2 * c + k)
        def _():
            for j in range(3):
                rx_copy(k, 1, j).wait_send()

    for k in range(4):
        for cc in range(2):

            @pl.when(jnp.logical_not(is_self(k, cc)))
            def _():
                ry_copy(k, cc).wait_send()


def per_device(inputs, weight, d_out):
    vmem, hbm = pl.BlockSpec(memory_space=pltpu.VMEM), pl.BlockSpec(memory_space=pltpu.HBM)
    dma = pltpu.SemaphoreType.DMA
    tokens, feats = inputs.shape
    return pl.pallas_call(
        kernel,
        out_shape=(
            jax.ShapeDtypeStruct((tokens, feats), BF),
            jax.ShapeDtypeStruct((B, B), F32),
        ),
        in_specs=[hbm, hbm, hbm],
        out_specs=(vmem, vmem),
        scratch_shapes=[
            pltpu.VMEM((tokens, feats), BF),
            pltpu.VMEM((B, B), BF),
            pltpu.VMEM((tokens, 128), BF),
            pltpu.VMEM((NM, B, 128), BF),
            pltpu.VMEM((NY, NZL, NC, B, CH), BF),
            pltpu.VMEM((tokens, CH), F32),
            pltpu.VMEM((tokens, CH), BF),
            pltpu.VMEM((tokens, CH), BF),
            pltpu.VMEM((4, CH, tokens), BF),
            pltpu.VMEM((4, CH, tokens), BF),
            pltpu.VMEM((4, CH, tokens), BF),
            pltpu.VMEM((4, 4, 2 * B, CH), BF),
            pltpu.VMEM((4, 3, 2 * B, CH), BF),
            pltpu.VMEM((3, 2 * B, CH), BF),
            pltpu.VMEM((3, 4, 2 * B, CH), BF),
            pltpu.VMEM((4, NC, B, CH), BF),
            pltpu.VMEM((NY, B, CH), BF),
            pltpu.VMEM((NM, B, 128), BF),
            pltpu.VMEM((NM, B, 128), BF),
            dma((3,)),
            dma((8,)), dma((8,)),
            dma((8,)), dma((8,)),
            dma((8, 3)), dma((8, 3)),
            dma((4, 3)), dma((4, 3)),
            dma((8,)), dma((8,)),
            dma, dma,
            dma, dma,
            dma((2, 3)), dma((4, 3)),
            dma((4, 3)), dma((4, 3)),
            dma((4, 2)), dma((8,)),
            dma((8,)), dma((8,)),
        ],
        compiler_params=pltpu.CompilerParams(
            collective_id=0, has_side_effects=True, vmem_limit_bytes=54_500_000
        ),
        name="attention_head_back",
    )(inputs, weight, d_out)


def solution(mesh):
    in_specs = (P(("dp", "mp"), None), P("dp", "mp"), P(("dp", "mp"), None))
    out_specs = (P(("dp", "mp"), None), P("dp", "mp"))
    return jax.shard_map(
        per_device, mesh=mesh, in_specs=in_specs, out_specs=out_specs, check_vma=False
    )
```

```python
import jax
import jax.numpy as jnp
from jax import lax
from jax.experimental import pallas as pl
from jax.experimental.pallas import tpu as pltpu
from jax.sharding import PartitionSpec as P

MESH = pl.DeviceIdType.MESH
BF = jnp.bfloat16
F32 = jnp.float32

NY, NZL, NC, NM = 8, 4, 2, 8
B = 48
PK = 32
CH = 384
STEPS = (0, 1, 7, 2, 6, 3, 5, 4)


def dot(a, b):
    return jnp.dot(a, b, preferred_element_type=F32)


def dot_nt(a, b):
    return lax.dot_general(a, b, (((1,), (1,)), ((), ())), preferred_element_type=F32)


def dot_tn(a, b):
    return lax.dot_general(a, b, (((0,), (0,)), ((), ())), preferred_element_type=F32)


def packed(a):
    low = jnp.concatenate([a[PK:], jnp.zeros((2 * PK - B, B), a.dtype)], axis=0)
    pad = jnp.zeros((PK, 128 - 2 * B), a.dtype)
    return jnp.concatenate([a[:PK], low, pad], axis=1)


def attention_back(qkv, d_out):
    hd = 128
    scale = hd**-0.5
    q, k, v = qkv[:, :hd], qkv[:, hd : 2 * hd], qkv[:, 2 * hd :]
    scores = dot_nt(q, k) * scale
    e = jnp.exp(scores - jnp.max(scores, axis=-1, keepdims=True))
    probs = e / jnp.sum(e, axis=-1, keepdims=True)
    grad_v = dot_tn(probs.astype(BF), d_out)
    grad_p = dot_nt(d_out, v)
    delta = jnp.sum(probs * grad_p, axis=-1, keepdims=True)
    grad_s = (probs * (grad_p - delta)).astype(BF)
    grad_q = dot(grad_s, k) * scale
    grad_k = dot_tn(grad_s, q) * scale
    return grad_q.astype(BF), grad_k.astype(BF), grad_v.astype(BF)


def kernel(
    inputs_hbm, weight_hbm, d_out_hbm, gi, wg_out,
    inputs, weight, d_out, wm, w, acc, g_own, g_other, t_own, t_send, t_other,
    part, rx, sx, rz, s2, ry, sm, rm,
    in_sem, wm_s, wm_r, y_s, y_r, z_s, z_r, x_s, x_r, c_s, c_r, t_s, t_r, g_s, g_r,
    rx_s, rx_r, rz_s, rz_r, ry_s, ry_r, rm_s, rm_r,
):
    dp, mp = lax.axis_index("dp"), lax.axis_index("mp")
    y, zl, c = dp // 8, (dp // 2) % 4, dp % 2
    zh, x = mp // 4, mp % 4
    z = zh * 4 + zl
    oc = 1 - c

    load_w = pltpu.make_async_copy(weight_hbm, weight, in_sem.at[0])
    load_w.start()
    load = pltpu.make_async_copy(inputs_hbm, inputs, in_sem.at[1])
    load.start()
    load_d = pltpu.make_async_copy(d_out_hbm, d_out, in_sem.at[2])
    load_d.start()

    def at(yy, zz, cc):
        return ((yy * 4 + zz % 4) * 2 + cc, (zz // 4) * 4 + x)

    def mp_peer(j):
        return (dp, (mp + j) % 8)

    def y_peer(d, cc):
        return at((y + d) % 8, z, cc)

    far = 2 - 4 * c
    z_steps = (1, -1, far)

    def z_peer(j, sign=1):
        return at(y, (z + sign * z_steps[j] + 8) % 8, c)

    def x_peer(p):
        return (dp, zh * 4 + (x + p) % 4)

    core_peer = at(y, z, oc)

    barrier = pltpu.get_barrier_semaphore()
    peers = [mp_peer(j) for j in range(1, 8)]
    peers += [y_peer(d, c) for d in range(1, 8)]
    peers += [y_peer(d, oc) for d in range(0, 8)]
    peers += [at(y, (z + dz + 8) % 8, c) for dz in (1, -1, 2, -2)]
    for peer in peers:
        pl.semaphore_signal(barrier, inc=1, device_id=peer, device_id_type=MESH)
    load_w.wait()
    wm[mp] = packed(weight[...])
    pl.semaphore_wait(barrier, len(peers))

    def remote(src, dst, ssem, rsem, peer):
        return pltpu.make_async_remote_copy(
            src_ref=src, dst_ref=dst, send_sem=ssem, recv_sem=rsem,
            device_id=peer, device_id_type=MESH,
        )

    def wm_copy(j, slot):
        return remote(wm.at[slot], wm.at[slot], wm_s.at[j], wm_r.at[j], mp_peer(j))

    for j in (6, 5, 7, 4, 2, 1, 3):
        wm_copy(j, mp).start()

    load.wait()
    load_d.wait()

    def chunk_of(k, half):
        return half * 4 + (k + y) % 4

    def columns(ch):
        return pl.ds(pl.multiple_of(ch * CH, CH), CH)

    for k in range(4):
        t_send[k] = inputs[:, columns(chunk_of(k, oc))].T
    t_copy = remote(t_send, t_other, t_s, t_r, core_peer)
    t_copy.start()

    for j in range(1, 8):
        wm_copy(j, (mp - j + 8) % 8).wait_recv()
    w[y, zl, c, :PK] = jnp.concatenate([wm[m, :, :B] for m in range(NM)], axis=1)
    w[y, zl, c, PK:] = jnp.concatenate([wm[m, : B - PK, B : 2 * B] for m in range(NM)], axis=1)

    def y_copy(d, src_y):
        blk = w.at[src_y, zl, c]
        return remote(blk, blk, y_s.at[d], y_r.at[d], y_peer(d, c))

    def z_copy(k, j, src_y, src_zl):
        blk = w.at[src_y, src_zl, c]
        return remote(blk, blk, z_s.at[k, j], z_r.at[k, j], z_peer(j))

    def c_copy(k, src_y, cc):
        blk = w.at[src_y, :, cc]
        return remote(blk, blk, c_s.at[k], c_r.at[k], core_peer)

    def x_copy(p, j, src_y, src_zl):
        blk = w.at[src_y, src_zl, c]
        return remote(blk, blk, x_s.at[p, j], x_r.at[p, j], x_peer(p))

    for k in range(1, 4):

        @pl.when(x == k)
        def _():
            y_copy(STEPS[k], y).start()

    for k in range(4, 8):
        y_copy(STEPS[k], y).start()
    ys = [(y - d + 8) % 8 for d in STEPS]
    zls = [(zl - s + 8) % 4 for s in z_steps]

    def shared_y(xx):
        return (y - jnp.where(xx == 2, 7, jnp.where(xx == 3, 2, xx)) + 8) % 8

    my_shared = shared_y(x)
    for k in range(1, 4):

        @pl.when(x == k)
        def _():
            y_copy(STEPS[k], ys[k]).wait_recv()
            for p in (2, 1, 3):
                x_copy(p, 3, my_shared, zl).start()

    for j in (2, 0, 1):
        z_copy(0, j, my_shared, zl).start()
    for k in range(4, 8):
        y_copy(STEPS[k], ys[k]).wait_recv()
        for j in (2, 0, 1):
            z_copy(k, j, ys[k], zl).start()
    for j in (0, 1, 2):
        z_copy(0, j, my_shared, zls[j]).wait_recv()
        for p in (2, 1, 3):
            x_copy(p, j, my_shared, zls[j]).start()
    for k in range(4):
        t_own[k] = inputs[:, columns(chunk_of(k, c))].T

    x_from = [(x - p + 4) % 4 for p in (1, 2, 3)]
    order = [(x, my_shared), (4, ys[4]), (5, ys[5])]
    order += [(xx, shared_y(xx)) for xx in x_from]
    order += [(6, ys[6]), (7, ys[7])]

    def multiply(n):
        k, yy = order[n]
        c_copy(k, yy, oc).wait_recv()
        p = dot(inputs[:, columns(yy)], w[yy].reshape(CH, CH))
        if n == 0:
            acc[...] = p
        else:
            acc[...] += p

    for n in range(8):
        k, yy = order[n]
        if n in (1, 2, 6, 7):
            for j in range(3):
                z_copy(k, j, yy, zls[j]).wait_recv()
        if n in (3, 4, 5):
            for j in range(3):
                x_copy(n - 2, j, yy, zls[j]).wait_recv()

            @pl.when(x_from[n - 3] != 0)
            def _():
                x_copy(n - 2, 3, yy, zl).wait_recv()

        c_copy(k, yy, c).start()
        if n > 3:
            multiply(n - 4)
    for n in range(4, 8):
        multiply(n)

    gq, gk, gv = attention_back(acc[...].astype(BF), d_out[...])
    g_own[:, :128] = gq
    g_own[:, 128:256] = gk
    g_own[:, 256:] = gv
    g_copy = remote(g_own, g_other, g_s, g_r, core_peer)
    g_copy.start()
    t_copy.wait_recv()
    g_copy.wait_recv()

    dest_zl = [(zl + s + 4) % 4 for s in z_steps]
    owner = x // 2 == c
    mine = x % 2

    def rx_copy(k, p, j):
        to = dest_zl[j]
        return remote(
            part.at[k, to], rx.at[p, j], rx_s.at[k, j], rx_r.at[p, j], x_peer(p)
        )

    def rz_copy(k, j):
        src = sx.at[j] if k == 0 else part.at[k, dest_zl[j]]
        return remote(src, rz.at[j, k], rz_s.at[k, j], rz_r.at[k, j], z_peer(j))

    def ry_copy(k, cc):
        return remote(
            s2.at[k, cc], ry.at[y], ry_s.at[k, cc], ry_r.at[y],
            at(chunk_of(k, c), z, cc),
        )

    def is_self(k, cc):
        return jnp.logical_and(chunk_of(k, c) == y, cc == c)

    def send_y(k, total):
        s2[k] = total.reshape(2, B, CH)
        for cc in range(2):
            self_k = is_self(k, cc)

            @pl.when(self_k)
            def _():
                ry[y] = s2[k, cc]

            @pl.when(jnp.logical_not(self_k))
            def _():
                ry_copy(k, cc).start()

    for k in range(4):
        p = dot(t_own[k], g_own[...]) + dot(t_other[k], g_other[...])
        part[k] = p.astype(BF).reshape(4, 2 * B, CH)
        if k < 2:
            to_owner = (2 * c + k - x + 4) % 4

            @pl.when(to_owner != 0)
            def _():
                for j in (2, 0, 1):
                    rx_copy(k, to_owner, j).start()
        else:
            for j in (2, 0, 1):
                rz_copy(k, j).start()
    for k in range(2):

        @pl.when(x != 2 * c + k)
        def _():
            send_y(k, part[k, zl])

    def grad_inputs(i):
        gi[:, i * CH : (i + 1) * CH] = dot_nt(g_own[...], w[i].reshape(CH, CH)).astype(BF)

    for i in range(4):
        grad_inputs(i)
    for n, j in enumerate((2, 0, 1)):

        @pl.when(owner)
        def _():
            total = part[mine, dest_zl[j]].astype(F32)
            for p in (1, 2, 3):
                rx_copy(0, p, j).wait_recv()
                total += rx[p, j].astype(F32)
            sx[j] = total.astype(BF)
            rz_copy(0, j).start()

        grad_inputs(4 + n)
    grad_inputs(7)

    def from_z(k, total):
        for j in range(3):
            rz_copy(k, j).wait_recv()
            total += rz[j, k].astype(F32)
        return total.astype(BF)

    for k in (2, 3):
        send_y(k, from_z(k, part[k, zl].astype(F32)))

    @pl.when(owner)
    def _():
        total = from_z(0, part[mine, zl].astype(F32))
        for k in range(2):

            @pl.when(mine == k)
            def _():
                send_y(k, total)

    src_core = y // 4
    for i in range(8):

        @pl.when(jnp.logical_not(jnp.logical_and(i == y, src_core == c)))
        def _():
            remote(s2.at[0, 0], ry.at[i], ry_s.at[0, 0], ry_r.at[i], core_peer).wait_recv()

    total = ry[0].astype(F32)
    for i in range(1, 8):
        total += ry[i].astype(F32)

    def rm_copy(j, to, slot):
        return remote(sm.at[to], rm.at[slot], rm_s.at[j], rm_r.at[j], mp_peer(j))

    for m in range(NM):
        sm[m] = packed(total[:, m * B : (m + 1) * B].astype(BF))
    for j in (6, 5, 7, 4, 2, 1, 3):
        rm_copy(j, (mp + j) % 8, mp).start()
    result = sm[mp].astype(F32)
    for j in range(1, 8):
        rm_copy(j, 0, (mp - j + 8) % 8).wait_recv()
        result += rm[(mp - j + 8) % 8].astype(F32)
    wg_out[:PK] = result[:, :B]
    wg_out[PK:] = result[: B - PK, B : 2 * B]

    for j in range(1, 8):
        wm_copy(j, mp).wait_send()
        rm_copy(j, 0, mp).wait_send()
    for j in range(3):
        for k in (0, 4, 5, 6, 7):
            z_copy(k, j, ys[k], zl).wait_send()
        for p in (1, 2, 3):
            x_copy(p, j, y, zl).wait_send()
        for k in (2, 3):
            rz_copy(k, j).wait_send()
    for k in range(1, 4):

        @pl.when(x == k)
        def _():
            y_copy(STEPS[k], y).wait_send()
            for p in (1, 2, 3):
                x_copy(p, 3, y, zl).wait_send()

    for k in range(4, 8):
        y_copy(STEPS[k], y).wait_send()
    for k in range(8):
        c_copy(k, ys[k], c).wait_send()
    t_copy.wait_send()
    g_copy.wait_send()

    @pl.when(owner)
    def _():
        for j in range(3):
            rz_copy(0, j).wait_send()

    for k in range(2):

        @pl.when(x != 2 * c + k)
        def _():
            for j in range(3):
                rx_copy(k, 1, j).wait_send()

    for k in range(4):
        for cc in range(2):

            @pl.when(jnp.logical_not(is_self(k, cc)))
            def _():
                ry_copy(k, cc).wait_send()


def per_device(inputs, weight, d_out):
    vmem, hbm = pl.BlockSpec(memory_space=pltpu.VMEM), pl.BlockSpec(memory_space=pltpu.HBM)
    dma = pltpu.SemaphoreType.DMA
    tokens, feats = inputs.shape
    inputs, weight, d_out = (
        pltpu.with_memory_space_constraint(a, pltpu.HBM) for a in (inputs, weight, d_out)
    )
    return pl.pallas_call(
        kernel,
        out_shape=(
            jax.ShapeDtypeStruct((tokens, feats), BF),
            jax.ShapeDtypeStruct((B, B), F32),
        ),
        in_specs=[hbm, hbm, hbm],
        out_specs=(vmem, vmem),
        scratch_shapes=[
            pltpu.VMEM((tokens, feats), BF),
            pltpu.VMEM((B, B), BF),
            pltpu.VMEM((tokens, 128), BF),
            pltpu.VMEM((NM, PK, 128), BF),
            pltpu.VMEM((NY, NZL, NC, B, CH), BF),
            pltpu.VMEM((tokens, CH), F32),
            pltpu.VMEM((tokens, CH), BF),
            pltpu.VMEM((tokens, CH), BF),
            pltpu.VMEM((4, CH, tokens), BF),
            pltpu.VMEM((4, CH, tokens), BF),
            pltpu.VMEM((4, CH, tokens), BF),
            pltpu.VMEM((4, 4, 2 * B, CH), BF),
            pltpu.VMEM((4, 3, 2 * B, CH), BF),
            pltpu.VMEM((3, 2 * B, CH), BF),
            pltpu.VMEM((3, 4, 2 * B, CH), BF),
            pltpu.VMEM((4, NC, B, CH), BF),
            pltpu.VMEM((NY, B, CH), BF),
            pltpu.VMEM((NM, PK, 128), BF),
            pltpu.VMEM((NM, PK, 128), BF),
            dma((3,)),
            dma((8,)), dma((8,)),
            dma((8,)), dma((8,)),
            dma((8, 3)), dma((8, 3)),
            dma((4, 4)), dma((4, 4)),
            dma((8,)), dma((8,)),
            dma, dma,
            dma, dma,
            dma((2, 3)), dma((4, 3)),
            dma((4, 3)), dma((4, 3)),
            dma((4, 2)), dma((8,)),
            dma((8,)), dma((8,)),
        ],
        compiler_params=pltpu.CompilerParams(
            collective_id=0, has_side_effects=True, vmem_limit_bytes=54_500_000
        ),
        name="attention_head_back",
    )(inputs, weight, d_out)


def solution(mesh):
    in_specs = (P(("dp", "mp"), None), P("dp", "mp"), P(("dp", "mp"), None))
    out_specs = (P(("dp", "mp"), None), P("dp", "mp"))
    return jax.shard_map(
        per_device, mesh=mesh, in_specs=in_specs, out_specs=out_specs, check_vma=False
    )
```

```python
import jax
import jax.numpy as jnp
from jax import lax
from jax.experimental import pallas as pl
from jax.experimental.pallas import tpu as pltpu
from jax.sharding import PartitionSpec as P

MESH = pl.DeviceIdType.MESH
BF = jnp.bfloat16
F32 = jnp.float32

NY, NZL, NC, NM = 8, 4, 2, 8
B = 48
PK = 32
CH = 384
STEPS = (0, 1, 7, 2, 4, 3, 5, 6)


def dot(a, b):
    return jnp.dot(a, b, preferred_element_type=F32)


def dot_nt(a, b):
    return lax.dot_general(a, b, (((1,), (1,)), ((), ())), preferred_element_type=F32)


def dot_tn(a, b):
    return lax.dot_general(a, b, (((0,), (0,)), ((), ())), preferred_element_type=F32)


def packed(a):
    low = jnp.concatenate([a[PK:], jnp.zeros((2 * PK - B, B), a.dtype)], axis=0)
    pad = jnp.zeros((PK, 128 - 2 * B), a.dtype)
    return jnp.concatenate([a[:PK], low, pad], axis=1)


def attention_back(qkv, d_out):
    hd = 128
    scale = hd**-0.5
    q, k, v = qkv[:, :hd], qkv[:, hd : 2 * hd], qkv[:, 2 * hd :]
    scores = dot_nt(q, k) * scale
    e = jnp.exp(scores - jnp.max(scores, axis=-1, keepdims=True))
    probs = e / jnp.sum(e, axis=-1, keepdims=True)
    grad_v = dot_tn(probs.astype(BF), d_out)
    grad_p = dot_nt(d_out, v)
    delta = jnp.sum(probs * grad_p, axis=-1, keepdims=True)
    grad_s = (probs * (grad_p - delta)).astype(BF)
    grad_q = dot(grad_s, k) * scale
    grad_k = dot_tn(grad_s, q) * scale
    return grad_q.astype(BF), grad_k.astype(BF), grad_v.astype(BF)


def kernel(
    inputs_hbm, weight_hbm, d_out_hbm, gi, wg_out,
    inputs, weight, d_out, wm, w, acc, g_own, g_other, t_own, t_send, t_other,
    own, part, rx, sx, rz, s2, ry, sm, rm,
    in_sem, wm_s, wm_r, y_s, y_r, z_s, z_r, x_s, x_r, c_s, c_r, t_s, t_r, g_s, g_r,
    rx_s, rx_r, rz_s, rz_r, ry_s, ry_r, rm_s, rm_r,
):
    dp, mp = lax.axis_index("dp"), lax.axis_index("mp")
    y, zl, c = dp // 8, (dp // 2) % 4, dp % 2
    zh, x = mp // 4, mp % 4
    z = zh * 4 + zl
    oc = 1 - c

    load_w = pltpu.make_async_copy(weight_hbm, weight, in_sem.at[0])
    load_w.start()
    load = pltpu.make_async_copy(inputs_hbm, inputs, in_sem.at[1])
    load.start()
    load_d = pltpu.make_async_copy(d_out_hbm, d_out, in_sem.at[2])
    load_d.start()

    def at(yy, zz, cc):
        return ((yy * 4 + zz % 4) * 2 + cc, (zz // 4) * 4 + x)

    def mp_peer(j):
        return (dp, (mp + j) % 8)

    def y_peer(d, cc):
        return at((y + d) % 8, z, cc)

    far = 2 - 4 * c
    z_steps = (1, -1, far)

    def z_peer(j, sign=1):
        return at(y, (z + sign * z_steps[j] + 8) % 8, c)

    def x_peer(p):
        return (dp, zh * 4 + (x + p) % 4)

    core_peer = at(y, z, oc)

    barrier = pltpu.get_barrier_semaphore()
    peers = [mp_peer(j) for j in (6, 5, 7, 4, 2, 1, 3)]
    peers += [y_peer(d, c) for d in (4, 3, 5, 2, 6, 1, 7)]
    peers += [at(y, (z + dz + 8) % 8, c) for dz in (1, -1, 2, -2)]
    peers += [y_peer(d, oc) for d in range(0, 8)]
    for peer in peers:
        pl.semaphore_signal(barrier, inc=1, device_id=peer, device_id_type=MESH)
    load_w.wait()
    wm[mp] = packed(weight[...])
    pl.semaphore_wait(barrier, len(peers))

    def remote(src, dst, ssem, rsem, peer):
        return pltpu.make_async_remote_copy(
            src_ref=src, dst_ref=dst, send_sem=ssem, recv_sem=rsem,
            device_id=peer, device_id_type=MESH,
        )

    def wm_copy(j, slot):
        return remote(wm.at[slot], wm.at[slot], wm_s.at[j], wm_r.at[j], mp_peer(j))

    for j in (6, 5, 7, 4, 2, 1, 3):
        wm_copy(j, mp).start()

    load.wait()
    load_d.wait()

    def chunk_of(k, half):
        return half * 4 + (k + y) % 4

    def columns(ch):
        return pl.ds(pl.multiple_of(ch * CH, CH), CH)

    for k in range(4):
        t_send[k] = inputs[:, columns(chunk_of(k, oc))].T
    t_copy = remote(t_send, t_other, t_s, t_r, core_peer)
    t_copy.start()

    for j in range(1, 8):
        wm_copy(j, (mp - j + 8) % 8).wait_recv()
    w[y, zl, c, :PK] = jnp.concatenate([wm[m, :, :B] for m in range(NM)], axis=1)
    w[y, zl, c, PK:] = jnp.concatenate([wm[m, : B - PK, B : 2 * B] for m in range(NM)], axis=1)

    def y_copy(d, src_y):
        blk = w.at[src_y, zl, c]
        return remote(blk, blk, y_s.at[d], y_r.at[d], y_peer(d, c))

    def z_copy(k, j, src_y, src_zl):
        blk = w.at[src_y, src_zl, c]
        return remote(blk, blk, z_s.at[k, j], z_r.at[k, j], z_peer(j))

    def c_copy(k, src_y, cc):
        blk = w.at[src_y, :, cc]
        return remote(blk, blk, c_s.at[k], c_r.at[k], core_peer)

    def x_copy(p, j, src_y, src_zl):
        blk = w.at[src_y, src_zl, c]
        return remote(blk, blk, x_s.at[p, j], x_r.at[p, j], x_peer(p))

    for k in range(1, 4):

        @pl.when(x == k)
        def _():
            y_copy(STEPS[k], y).start()

    for k in range(4, 8):
        y_copy(STEPS[k], y).start()
    ys = [(y - d + 8) % 8 for d in STEPS]
    zls = [(zl - s + 8) % 4 for s in z_steps]

    def shared_y(xx):
        return (y - jnp.where(xx == 2, 7, jnp.where(xx == 3, 2, xx)) + 8) % 8

    my_shared = shared_y(x)
    for k in range(1, 4):

        @pl.when(x == k)
        def _():
            y_copy(STEPS[k], ys[k]).wait_recv()
            for p in (2, 1, 3):
                x_copy(p, 3, my_shared, zl).start()

    for j in (2, 0, 1):
        z_copy(0, j, my_shared, zl).start()
    for k in range(4, 8):
        y_copy(STEPS[k], ys[k]).wait_recv()
        for j in (2, 0, 1):
            z_copy(k, j, ys[k], zl).start()
    for j in (0, 1, 2):
        z_copy(0, j, my_shared, zls[j]).wait_recv()
        for p in (2, 1, 3):
            x_copy(p, j, my_shared, zls[j]).start()
    for k in range(4):
        t_own[k] = inputs[:, columns(chunk_of(k, c))].T

    x_from = [(x - p + 4) % 4 for p in (1, 2, 3)]
    order = [(x, my_shared), (4, ys[4]), (5, ys[5])]
    order += [(xx, shared_y(xx)) for xx in x_from]
    order += [(6, ys[6]), (7, ys[7])]

    def multiply(n):
        k, yy = order[n]
        c_copy(k, yy, oc).wait_recv()
        p = dot(inputs[:, columns(yy)], w[yy].reshape(CH, CH))
        if n == 0:
            acc[...] = p
        else:
            acc[...] += p

    for n in range(8):
        k, yy = order[n]
        if n in (1, 2, 6, 7):
            for j in range(3):
                z_copy(k, j, yy, zls[j]).wait_recv()
        if n in (3, 4, 5):
            for j in range(3):
                x_copy(n - 2, j, yy, zls[j]).wait_recv()

            @pl.when(x_from[n - 3] != 0)
            def _():
                x_copy(n - 2, 3, yy, zl).wait_recv()

        c_copy(k, yy, c).start()
        if n > 3:
            multiply(n - 4)
    for n in range(4, 8):
        multiply(n)

    gq, gk, gv = attention_back(acc[...].astype(BF), d_out[...])
    g_own[:, :128] = gq
    g_own[:, 128:256] = gk
    g_own[:, 256:] = gv
    g_copy = remote(g_own, g_other, g_s, g_r, core_peer)
    g_copy.start()
    for k in range(4):
        own[k] = dot(t_own[k], g_own[...])
    t_copy.wait_recv()
    g_copy.wait_recv()

    dest_zl = [(zl + s + 4) % 4 for s in z_steps]
    owner = x // 2 == c
    mine = x % 2

    def rx_copy(k, p, j):
        to = dest_zl[j]
        return remote(
            part.at[k, to], rx.at[p, j], rx_s.at[k, j], rx_r.at[p, j], x_peer(p)
        )

    def rz_copy(k, j):
        src = sx.at[j] if k == 0 else part.at[k, dest_zl[j]]
        return remote(src, rz.at[j, k], rz_s.at[k, j], rz_r.at[k, j], z_peer(j))

    def ry_copy(k, cc):
        return remote(
            s2.at[k, cc], ry.at[y], ry_s.at[k, cc], ry_r.at[y],
            at(chunk_of(k, c), z, cc),
        )

    def is_self(k, cc):
        return jnp.logical_and(chunk_of(k, c) == y, cc == c)

    def send_y(k, total):
        s2[k] = total.reshape(2, B, CH)
        for cc in range(2):
            self_k = is_self(k, cc)

            @pl.when(self_k)
            def _():
                ry[y] = s2[k, cc]

            @pl.when(jnp.logical_not(self_k))
            def _():
                ry_copy(k, cc).start()

    for k in range(4):
        p = own[k] + dot(t_other[k], g_other[...])
        part[k] = p.astype(BF).reshape(4, 2 * B, CH)
        if k < 2:
            to_owner = (2 * c + k - x + 4) % 4

            @pl.when(to_owner != 0)
            def _():
                for j in (2, 0, 1):
                    rx_copy(k, to_owner, j).start()
        else:
            for j in (2, 0, 1):
                rz_copy(k, j).start()
    for k in range(2):

        @pl.when(x != 2 * c + k)
        def _():
            send_y(k, part[k, zl])

    def grad_inputs(i):
        gi[:, i * CH : (i + 1) * CH] = dot_nt(g_own[...], w[i].reshape(CH, CH)).astype(BF)

    for i in range(4):
        grad_inputs(i)
    for n, j in enumerate((2, 0, 1)):

        @pl.when(owner)
        def _():
            total = part[mine, dest_zl[j]].astype(F32)
            for p in (1, 2, 3):
                rx_copy(0, p, j).wait_recv()
                total += rx[p, j].astype(F32)
            sx[j] = total.astype(BF)
            rz_copy(0, j).start()

        grad_inputs(4 + n)
    grad_inputs(7)

    def from_z(k, total):
        for j in range(3):
            rz_copy(k, j).wait_recv()
            total += rz[j, k].astype(F32)
        return total.astype(BF)

    for k in (2, 3):
        send_y(k, from_z(k, part[k, zl].astype(F32)))

    @pl.when(owner)
    def _():
        total = from_z(0, part[mine, zl].astype(F32))
        for k in range(2):

            @pl.when(mine == k)
            def _():
                send_y(k, total)

    src_core = y // 4
    for i in range(8):

        @pl.when(jnp.logical_not(jnp.logical_and(i == y, src_core == c)))
        def _():
            remote(s2.at[0, 0], ry.at[i], ry_s.at[0, 0], ry_r.at[i], core_peer).wait_recv()

    total = ry[0].astype(F32)
    for i in range(1, 8):
        total += ry[i].astype(F32)

    def rm_copy(j, to, slot):
        return remote(sm.at[to], rm.at[slot], rm_s.at[j], rm_r.at[j], mp_peer(j))

    for m in range(NM):
        sm[m] = packed(total[:, m * B : (m + 1) * B].astype(BF))
    for j in (6, 5, 7, 4, 2, 1, 3):
        rm_copy(j, (mp + j) % 8, mp).start()
    result = sm[mp].astype(F32)
    for j in range(1, 8):
        rm_copy(j, 0, (mp - j + 8) % 8).wait_recv()
        result += rm[(mp - j + 8) % 8].astype(F32)
    wg_out[:PK] = result[:, :B]
    wg_out[PK:] = result[: B - PK, B : 2 * B]

    for j in range(1, 8):
        wm_copy(j, mp).wait_send()
        rm_copy(j, 0, mp).wait_send()
    for j in range(3):
        for k in (0, 4, 5, 6, 7):
            z_copy(k, j, ys[k], zl).wait_send()
        for p in (1, 2, 3):
            x_copy(p, j, y, zl).wait_send()
        for k in (2, 3):
            rz_copy(k, j).wait_send()
    for k in range(1, 4):

        @pl.when(x == k)
        def _():
            y_copy(STEPS[k], y).wait_send()
            for p in (1, 2, 3):
                x_copy(p, 3, y, zl).wait_send()

    for k in range(4, 8):
        y_copy(STEPS[k], y).wait_send()
    for k in range(8):
        c_copy(k, ys[k], c).wait_send()
    t_copy.wait_send()
    g_copy.wait_send()

    @pl.when(owner)
    def _():
        for j in range(3):
            rz_copy(0, j).wait_send()

    for k in range(2):

        @pl.when(x != 2 * c + k)
        def _():
            for j in range(3):
                rx_copy(k, 1, j).wait_send()

    for k in range(4):
        for cc in range(2):

            @pl.when(jnp.logical_not(is_self(k, cc)))
            def _():
                ry_copy(k, cc).wait_send()


WRITES = 4


def write_out(gi, wg, gi_hbm, wg_hbm, sems):
    rows = gi.shape[0] // WRITES
    copies = [pltpu.make_async_copy(wg, wg_hbm, sems.at[WRITES])]
    for i in range(WRITES):
        part = pl.ds(i * rows, rows)
        copies.append(pltpu.make_async_copy(gi.at[part], gi_hbm.at[part], sems.at[i]))
    for copy in copies:
        copy.start()
    for copy in copies:
        copy.wait()


def per_device(inputs, weight, d_out):
    vmem, hbm = pl.BlockSpec(memory_space=pltpu.VMEM), pl.BlockSpec(memory_space=pltpu.HBM)
    dma = pltpu.SemaphoreType.DMA
    tokens, feats = inputs.shape
    inputs, weight, d_out = (
        pltpu.with_memory_space_constraint(a, pltpu.HBM) for a in (inputs, weight, d_out)
    )
    grad_inputs, weight_grad = pl.pallas_call(
        kernel,
        out_shape=(
            jax.ShapeDtypeStruct((tokens, feats), BF),
            jax.ShapeDtypeStruct((B, B), F32),
        ),
        in_specs=[hbm, hbm, hbm],
        out_specs=(vmem, vmem),
        scratch_shapes=[
            pltpu.VMEM((tokens, feats), BF),
            pltpu.VMEM((B, B), BF),
            pltpu.VMEM((tokens, 128), BF),
            pltpu.VMEM((NM, PK, 128), BF),
            pltpu.VMEM((NY, NZL, NC, B, CH), BF),
            pltpu.VMEM((tokens, CH), F32),
            pltpu.VMEM((tokens, CH), BF),
            pltpu.VMEM((tokens, CH), BF),
            pltpu.VMEM((4, CH, tokens), BF),
            pltpu.VMEM((4, CH, tokens), BF),
            pltpu.VMEM((4, CH, tokens), BF),
            pltpu.VMEM((4, CH, CH), F32),
            pltpu.VMEM((4, 4, 2 * B, CH), BF),
            pltpu.VMEM((4, 3, 2 * B, CH), BF),
            pltpu.VMEM((3, 2 * B, CH), BF),
            pltpu.VMEM((3, 4, 2 * B, CH), BF),
            pltpu.VMEM((4, NC, B, CH), BF),
            pltpu.VMEM((NY, B, CH), BF),
            pltpu.VMEM((NM, PK, 128), BF),
            pltpu.VMEM((NM, PK, 128), BF),
            dma((3,)),
            dma((8,)), dma((8,)),
            dma((8,)), dma((8,)),
            dma((8, 3)), dma((8, 3)),
            dma((4, 4)), dma((4, 4)),
            dma((8,)), dma((8,)),
            dma, dma,
            dma, dma,
            dma((2, 3)), dma((4, 3)),
            dma((4, 3)), dma((4, 3)),
            dma((4, 2)), dma((8,)),
            dma((8,)), dma((8,)),
        ],
        compiler_params=pltpu.CompilerParams(
            collective_id=0, has_side_effects=True, vmem_limit_bytes=54_500_000
        ),
        name="attention_head_back",
    )(inputs, weight, d_out)
    anywhere = pl.BlockSpec(memory_space=pl.ANY)
    return pl.pallas_call(
        write_out,
        out_shape=(
            jax.ShapeDtypeStruct((tokens, feats), BF),
            jax.ShapeDtypeStruct((B, B), F32),
        ),
        in_specs=[anywhere, anywhere],
        out_specs=(anywhere, anywhere),
        scratch_shapes=[dma((WRITES + 1,))],
        compiler_params=pltpu.CompilerParams(vmem_limit_bytes=1 << 20),
        name="write_out",
    )(grad_inputs, weight_grad)


def solution(mesh):
    in_specs = (P(("dp", "mp"), None), P("dp", "mp"), P(("dp", "mp"), None))
    out_specs = (P(("dp", "mp"), None), P("dp", "mp"))
    return jax.shard_map(
        per_device, mesh=mesh, in_specs=in_specs, out_specs=out_specs, check_vma=False
    )
```
